32 devices in a mesh: gx: 4 (over z), gy: 8 (over y, x, core).
Axes of the slice: x: 2, y: 2, z: 4, core: 2. Of those that a mesh axis runs over, the one named last changes fastest.
Arguments:
- inputs: bfloat16 [8192, 1024], P(('gx', 'gy')), may hold values from -6 to 6
- first_weight: bfloat16 [1024, 1024], replicated, may hold values from -0.1875 to 0.1875
- second_weight: bfloat16 [1024, 512], replicated, may hold values from -0.1875 to 0.1875
- targets: bfloat16 [8192], P(('gx', 'gy')), may hold values from -6 to 6
- noise_var: float32 [32], P(('gx', 'gy')), may hold values from 0.5 to 4
- assignment: int32 [8192, 1], P(('gx', 'gy')), may hold values from 0 to 31; in each aligned block of 256 rows (0 to 255, 256 to 511, ...) at most 16 rows name the same one
Outputs:
- grad_first: float32 [1024, 1024], P(('gx', 'gy'))
- grad_second: float32 [1024, 512], P(('gx', 'gy'))
- expert_loss: float32 [32], P(('gx', 'gy'))
The draws below stay inside these ranges and needn't reach their ends.
Inputs may be any that keep to these rules, and one draw needn't show every extreme that they name: `assignment`: the rows of one device name one expert at most 16 times; every expert is named by some row.
All inputs are finite; a program needn't handle non-finite values.
Results may differ from the reference program's by a relative error of at most 0.0033.
Values may be sent and summed in bfloat16 or wider, within the bound.
No kernel may reach another device: no remote copies, remote signals or barrier semaphores. Data moves between devices by JAX's collectives and lax.ppermute only.
A program may use at most 64 MiB of HBM per device.

```python
import math
import jax
import jax.numpy as jnp
import numpy as np
from jax import lax

DIN = 1024
HID = 1024
FEAT = 512
CAP = 512
ITERS = 4
ROWS_DEV = 256
EXPERTS = 32
SLOT = 16
ROWS = 8192
N_GX = 4
N_GY = 8


def level_of(stream_key, dims, split, low, largest):
    level = 1.0
    for position, shards_of in split:
        steps = jax.random.uniform(jax.random.fold_in(jax.random.fold_in(stream_key, 6), position), (shards_of,), jnp.float32, low / len(split), largest / len(split))
        level = level * jnp.repeat(jnp.exp(steps), dims[position] // shards_of).reshape((-1,) + (1,) * (len(dims) - 1 - position))
    return level


def assign_block(rng, own, number, rows, amount, top, limit, skew):
    sequence = jax.random.permutation(rng, amount)
    crowded, usual = load_shares(amount, rows * top, limit, skew, True), load_shares(amount, rows * top, limit, skew, False)
    places = jnp.arange(amount)

    def named(lengths, offset_by):
        used = int((lengths > 0).sum())
        fixed = max(1, used // 4)
        passed = fixed + (places - fixed + offset_by * (used - fixed)) % max(1, amount - fixed)
        return jnp.zeros((amount,), jnp.int32).at[sequence[jnp.where(places < fixed, places, passed)]].set(jnp.asarray(lengths, jnp.int32))

    lengths = jnp.where(number % 4 == 0, named(crowded, number // 4), named(usual, number - number // 4 - 1))
    mixed = jax.random.permutation(jax.random.fold_in(own, 3), amount)
    donor, receiver = mixed[0:amount // 2 * 2:2], mixed[1:amount // 2 * 2:2]
    margin = jnp.minimum(lengths[donor] - 1, limit - lengths[receiver]) // 2
    margin = jnp.where((donor == sequence[0]) | (receiver == sequence[0]) | (lengths[receiver] == 0), 0, jnp.maximum(margin, 0))
    passed = jax.random.randint(jax.random.fold_in(own, 4), (amount // 2,), 0, 1 << 20) % (margin + 1)
    lengths = lengths.at[donor].add(-passed).at[receiver].add(passed)
    members = jnp.searchsorted(jnp.cumsum(lengths), jnp.arange(rows * top), side="right").astype(jnp.int32)
    grid = members.reshape(top, rows).T
    grid = grid[jax.random.permutation(jax.random.fold_in(own, 1), rows)]
    offset_by = jax.random.randint(jax.random.fold_in(own, 2), (rows, 1), 0, top)
    return jnp.take_along_axis(grid, (jnp.arange(top)[None, :] + offset_by) % top, axis=1)


def load_shares(amount, total, most, slope, full):
    weights = [(1 << 20) // math.isqrt(standing ** slope) + 1 for standing in range(1, amount + 1)]
    largest = most if full else min(most, max(-(-total // amount), total * weights[0] // sum(weights)))
    least = 1 if total - largest >= amount - 1 else 0
    given, rest = [largest] + [least] * (amount - 1), total - largest - least * (amount - 1)
    while rest > 0:
        free = [i for i in range(1, amount) if given[i] < largest] or [i for i in range(1, amount) if given[i] < most]
        whole, budget = sum([weights[i] for i in free]), rest
        for i in free:
            more = min(most - given[i], max(1, budget * weights[i] // whole), rest)
            given[i] = given[i] + more
            rest = rest - more
    return np.array(given)


def normal_values(key, shape, width, most, pieces=(), kind=jnp.bfloat16):
    entries = jax.random.normal(key, shape, jnp.float32) * width
    if len(pieces) > 0:
        entries = level_of(key, shape, pieces, -0.22, 0.18) * entries
    return jnp.clip(entries, min=-most, max=most).astype(kind)


def setup_inputs(seed: int = 0) -> dict:
    streams_of = jax.random.split(jax.random.key(seed), 7)
    inputs = normal_values(streams_of[0], (ROWS, DIN), 1.0, 6.0, ((0, 32),))
    first_weight = normal_values(streams_of[1], (DIN, HID), DIN ** -0.5, 0.1875)
    second_weight = normal_values(streams_of[2], (HID, FEAT), HID ** -0.5, 0.1875)
    targets = normal_values(streams_of[3], (ROWS,), 1.0, 6.0, ((0, 32),))
    noise_var = jnp.clip(jnp.exp(math.log(4.0) - 2.0794415 * jax.random.uniform(streams_of[4], (EXPERTS,), jnp.float32) ** level_of(streams_of[4], (EXPERTS,), ((0, 32),), -0.2, 0.2)), 0.5, 4.0)
    assignment_keys = jax.random.split(jax.random.fold_in(streams_of[5], 1), ROWS // ROWS_DEV)
    assignment_turns = jax.random.permutation(jax.random.fold_in(streams_of[5], 3), ROWS // ROWS_DEV)
    assignment = jax.vmap(lambda own, number: assign_block(jax.random.fold_in(streams_of[5], 2), own, number, ROWS_DEV, EXPERTS, 1, SLOT, 2))(assignment_keys, assignment_turns).reshape((ROWS, 1))
    return dict(inputs=inputs, first_weight=first_weight, second_weight=second_weight, targets=targets, noise_var=noise_var, assignment=assignment)


def gram_objective(gram_matrix, targets, noise):
    count = gram_matrix.shape[0]
    scale_bound = noise + jnp.sqrt(jnp.sum(gram_matrix * gram_matrix) + 1e-06)
    identity = jnp.eye(count, dtype=gram_matrix.dtype)
    kernel = gram_matrix + noise * identity
    approx = identity / scale_bound
    for sweep in range(ITERS):
        product = jnp.dot(kernel, approx, precision=lax.Precision.HIGHEST)
        approx = 2.0 * approx - jnp.dot(approx, product, precision=lax.Precision.HIGHEST)
    fitted = jnp.dot(approx, targets, precision=lax.Precision.HIGHEST)
    return 0.5 * jnp.sum(targets * fitted)

def one_expert(packed):
    feats, targs, noise = packed
    targs32 = targs.astype(jnp.float32)
    gram_matrix = jnp.dot(feats, feats.T, preferred_element_type=jnp.float32) / FEAT
    loss, pullback = jax.vjp(lambda g: gram_objective(g, targs32, noise), gram_matrix)
    gram_grad = pullback(jnp.ones((), loss.dtype))[0]
    grad_rows = jnp.dot(gram_grad + gram_grad.T, feats.astype(gram_grad.dtype), precision=lax.Precision.HIGHEST) / FEAT
    return (loss, grad_rows.astype(jnp.bfloat16))

def reference(inputs, first_weight, second_weight, targets, noise_var, assignment):
    devices = N_GX * N_GY
    per_slot = CAP // devices
    pre_act = jnp.dot(inputs, first_weight, preferred_element_type=jnp.float32)
    hidden = jax.nn.silu(pre_act).astype(jnp.bfloat16)
    features = jnp.dot(hidden, second_weight, preferred_element_type=jnp.float32).astype(jnp.bfloat16)
    assign = assignment[:, 0].astype(jnp.int32).reshape(devices, ROWS_DEV)
    onehot = (assign[:, :, None] == jnp.arange(EXPERTS, dtype=jnp.int32)[None, None, :]).astype(jnp.int32)
    row_rank = jnp.cumsum(onehot, axis=1) - onehot
    row_slot = lax.optimization_barrier(jnp.sum(row_rank * onehot, axis=2))
    source = jnp.arange(devices, dtype=jnp.int32)[:, None]
    row_index = (assign * CAP + source * per_slot + row_slot).reshape(-1).astype(jnp.int32)
    buffer = jnp.zeros((EXPERTS * CAP, FEAT), features.dtype).at[row_index].set(features)
    targ_buffer = jnp.zeros((EXPERTS * CAP,), targets.dtype).at[row_index].set(targets)
    expert_loss, grads = lax.map(one_expert, (buffer.reshape(EXPERTS, CAP, FEAT), targ_buffer.reshape(EXPERTS, CAP), noise_var))
    feat_grad = grads.reshape(EXPERTS * CAP, FEAT)[row_index]
    grad_second = jnp.dot(hidden.T, feat_grad, preferred_element_type=jnp.float32)
    hidden_grad = jnp.dot(feat_grad, second_weight.T, preferred_element_type=jnp.float32)
    sigma = jax.nn.sigmoid(pre_act)
    pre_grad = (hidden_grad * sigma * (1.0 + pre_act * (1.0 - sigma))).astype(jnp.bfloat16)
    grad_first = jnp.dot(inputs.T, pre_grad, preferred_element_type=jnp.float32)
    return (grad_first, grad_second, expert_loss)
```

```python
import functools

import jax
import jax.numpy as jnp
from jax import lax
from jax.experimental import pallas as pl
from jax.experimental.pallas import tpu as pltpu
from jax.sharding import PartitionSpec as P

CAP = 512
POWERS = 16
BF16 = jnp.bfloat16
F32 = jnp.float32
EXACT = lax.Precision.HIGHEST
VMEM = pl.BlockSpec(memory_space=pltpu.VMEM)
SMEM = pl.BlockSpec(memory_space=pltpu.SMEM)
PARAMS = pltpu.CompilerParams(vmem_limit_bytes=48 * 1024 * 1024)


def dot(left, right, left_dim=1, right_dim=0, precision=None):
    return lax.dot_general(
        left,
        right,
        (((left_dim,), (right_dim,)), ((), ())),
        preferred_element_type=F32,
        precision=precision,
    )


def iota(shape, dim):
    return lax.broadcasted_iota(jnp.int32, shape, dim)


def dispatch_kernel(devices, assign_ref, targ_ref, rows_ref, out_ref):
    assign = assign_ref[...]
    count, width = rows_ref.shape
    per_slot = CAP // devices
    onehot = iota((devices, count), 0) == assign
    earlier = (iota((count, count), 0) < iota((count, count), 1)).astype(BF16)
    rank = dot(onehot.astype(BF16), earlier)
    slot = jnp.sum(jnp.where(onehot, rank, 0.0), axis=0, keepdims=True)
    place = assign * per_slot + slot.astype(jnp.int32)
    here = iota((CAP, count), 0) == place
    out_ref[:, :width] = dot(here.astype(BF16), rows_ref[...]).astype(BF16)
    targ = jnp.sum(jnp.where(here, targ_ref[...].astype(F32), 0.0), axis=1, keepdims=True)
    out_ref[:, width:] = jnp.broadcast_to(targ, (CAP, 128)).astype(BF16)


def gram_rows_to_column(gram, row):
    parts = []
    for start in range(0, CAP, 64):
        product = gram[start : start + 64, :] * row
        folded = sum(product[:, lane : lane + 128] for lane in range(0, CAP, 128))
        parts.append(jnp.sum(folded, axis=1, keepdims=True))
    return jnp.concatenate(parts, axis=0)


def gram_column_to_row(gram, column):
    total = jnp.zeros((8, CAP), F32)
    for start in range(0, CAP, 64):
        product = gram[start : start + 64, :] * column[start : start + 64, :]
        total = total + jnp.sum(product.reshape(8, 8, CAP), axis=0)
    return jnp.sum(total, axis=0, keepdims=True)


def expert_kernel(
    blocks,
    parity_ref,
    noise_ref,
    got_ref,
    first_ref,
    second_ref,
    keep1_ref,
    send1_ref,
    keep2_ref,
    send2_ref,
    loss_ref,
    pre_ref,
    hid_ref,
    feat_ref,
    gram_ref,
    grad_ref,
    pgrad_ref,
    xt_ref,
    ht_ref,
):
    din, hid = first_ref.shape
    feat = second_ref.shape[1]
    step = 128
    chunks = CAP // step

    def split_parity(source, target):
        turned = source.T.reshape(blocks // 2, 2, din // blocks, CAP)
        target[0] = turned[:, 0].reshape(din // 2, CAP)
        target[1] = turned[:, 1].reshape(din // 2, CAP)

    @pl.loop(0, chunks)
    def _(i):
        rows = pl.ds(pl.multiple_of(i * step, step), step)
        pre = dot(got_ref[rows, :din], first_ref[...])
        pre_ref[rows, :] = pre
        hidden = (pre * jax.nn.sigmoid(pre)).astype(BF16)
        hid_ref[rows, :] = hidden
        feat_ref[rows, :] = dot(hidden, second_ref[...]).astype(BF16)

    split_parity(got_ref[:, :din], xt_ref)
    split_parity(hid_ref[...], ht_ref)

    feats = feat_ref[...]
    gram_ref[...] = dot(feats, feats, 1, 1) * (1.0 / feat)
    gram = gram_ref[...]
    noise = noise_ref[0]
    squares = sum(
        jnp.sum((gram[i : i + 64, :] * gram[i : i + 64, :]).reshape(8, 8, CAP), axis=0)
        for i in range(0, CAP, 64)
    )
    root = jnp.sqrt(jnp.sum(squares, keepdims=True) + 1e-06)
    theta = root + noise
    inverse = 1.0 / theta
    shrink = root * inverse

    targ = got_ref[:, din:].astype(F32)
    column = targ[:, :1]
    lane = iota((CAP, 128), 1)
    sub = iota((POWERS, CAP), 0)
    columns = jnp.where(lane == 0, targ, 0.0)
    row_set = jnp.zeros((POWERS, CAP), F32)
    targ_row = targ.T[:1, :]
    row = None
    previous_row = targ_row
    for k in range(1, POWERS - 1):
        if k % 2 == 1:
            before = previous_row if k == 1 else columns.T[k - 1 : k, :]
            row = shrink * before - gram_column_to_row(gram, column) * inverse
            row_set = row_set + jnp.where(sub == k, row, 0.0)
        else:
            before = row.T
            column = shrink * before - gram_rows_to_column(gram, row) * inverse
            columns = columns + jnp.where(lane == k, column, 0.0)
    powers = row_set + columns.T[:POWERS, :]
    moments = jnp.sum(powers * targ_row, axis=1, keepdims=True)
    last = jnp.sum(powers[7:8, :] * powers[8:9, :], axis=1, keepdims=True)
    loss_ref[...] = 0.5 * inverse * (jnp.sum(moments, axis=0, keepdims=True) + last)
    mask = (iota((POWERS, POWERS), 0) + iota((POWERS, POWERS), 1) <= POWERS - 2).astype(F32)
    sums = dot(mask, powers, precision=EXACT)
    outer = dot(powers, sums, 0, 0, precision=EXACT) + (16.0 * last / root) * gram
    high = outer.astype(BF16)
    low = (outer - high.astype(F32)).astype(BF16)
    scale = -inverse * inverse * (1.0 / feat)
    grad_ref[...] = ((dot(high, feats) + dot(low, feats)) * scale).astype(BF16)

    parity = parity_ref[0]
    keep2_ref[...] = dot(ht_ref[parity], grad_ref[...])
    send2_ref[...] = dot(ht_ref[1 - parity], grad_ref[...])

    @pl.loop(0, chunks)
    def _(i):
        rows = pl.ds(pl.multiple_of(i * step, step), step)
        hidden_grad = dot(grad_ref[rows, :], second_ref[...], 1, 1)
        pre = pre_ref[rows, :]
        sigma = jax.nn.sigmoid(pre)
        pgrad_ref[rows, :] = (hidden_grad * sigma * (1.0 + pre * (1.0 - sigma))).astype(BF16)

    keep1_ref[...] = dot(xt_ref[parity], pgrad_ref[...])
    send1_ref[...] = dot(xt_ref[1 - parity], pgrad_ref[...])


def split_kernel(group, count, place_ref, *refs):
    arrays, outs = refs[: -2 * group], refs[-2 * group :]
    place = place_ref[0]
    for which in range(2):
        parts = arrays[which * count : (which + 1) * count]
        for d in range(group):
            target = jnp.bitwise_xor(place, d)
            out = outs[which * group + d]
            total = parts[0][:, target].astype(F32)
            for part in parts[1:]:
                total = total + part[:, target].astype(F32)
            out[...] = total.astype(out.dtype)


def split_stage(place, first_parts, second_parts, group):
    def shapes(part):
        shape = (part.shape[0], *part.shape[2:])
        return [jax.ShapeDtypeStruct(shape, F32 if d == 0 else BF16) for d in range(group)]

    outs = shapes(first_parts[0]) + shapes(second_parts[0])
    made = pl.pallas_call(
        functools.partial(split_kernel, group, len(first_parts)),
        out_shape=outs,
        in_specs=[SMEM] + [VMEM] * (2 * len(first_parts)),
        out_specs=[VMEM] * (2 * group),
        compiler_params=PARAMS,
    )(place, *first_parts, *second_parts)
    return made[:group], made[group:]


def swap(array, axis, distance):
    count = lax.axis_size(axis)
    return lax.ppermute(array, axis, [(i, i ^ distance) for i in range(count)])


def exchange(parts, axis, unit):
    return [parts[0]] + [swap(parts[d], axis, d * unit) for d in range(1, len(parts))]


def on_device(inputs, first_weight, second_weight, targets, noise_var, assignment):
    gx_count = lax.axis_size("gx")
    gy_count = lax.axis_size("gy")
    devices = gx_count * gy_count
    per_slot = CAP // devices
    rows, din = inputs.shape
    hid, feat = second_weight.shape
    own_rows = din // devices
    gx = lax.axis_index("gx")
    gy = lax.axis_index("gy")

    def scalar(x):
        return x.astype(jnp.int32).reshape(1)

    sent = pl.pallas_call(
        functools.partial(dispatch_kernel, devices),
        out_shape=jax.ShapeDtypeStruct((CAP, din + 128), BF16),
        in_specs=[VMEM] * 3,
        out_specs=VMEM,
        compiler_params=PARAMS,
    )(assignment.reshape(1, rows), targets.reshape(1, rows), inputs)
    got = lax.all_to_all(
        sent.reshape(devices, per_slot, din + 128),
        ("gx", "gy"),
        split_axis=0,
        concat_axis=0,
        tiled=True,
    ).reshape(CAP, din + 128)

    half = din // 2
    keep1, send1, keep2, send2, loss = pl.pallas_call(
        functools.partial(expert_kernel, devices),
        out_shape=[
            jax.ShapeDtypeStruct((half, hid), F32),
            jax.ShapeDtypeStruct((half, hid), F32),
            jax.ShapeDtypeStruct((half, feat), F32),
            jax.ShapeDtypeStruct((half, feat), F32),
            jax.ShapeDtypeStruct((1, 1), F32),
        ],
        in_specs=[SMEM, SMEM, VMEM, VMEM, VMEM],
        out_specs=[VMEM] * 5,
        scratch_shapes=[
            pltpu.VMEM((CAP, hid), F32),
            pltpu.VMEM((CAP, hid), BF16),
            pltpu.VMEM((CAP, feat), BF16),
            pltpu.VMEM((CAP, CAP), F32),
            pltpu.VMEM((CAP, feat), BF16),
            pltpu.VMEM((CAP, hid), BF16),
            pltpu.VMEM((2, half, CAP), BF16),
            pltpu.VMEM((2, half, CAP), BF16),
        ],
        compiler_params=PARAMS,
    )(scalar(gy % 2), noise_var, got, first_weight, second_weight)

    plane = gy_count // 2
    got2 = swap(send2, "gy", 1)
    got1 = swap(send1, "gy", 1)

    def cut(array, outer, group):
        return array.reshape(outer, group, own_rows, array.shape[-1])

    first_parts, second_parts = split_stage(
        scalar(gy // 2),
        [cut(a, gx_count, plane) for a in (keep1, got1)],
        [cut(a, gx_count, plane) for a in (keep2, got2)],
        plane,
    )
    second_parts = exchange(second_parts, "gy", 2)
    first_parts = exchange(first_parts, "gy", 2)
    first_parts, second_parts = split_stage(
        scalar(gx),
        [cut(a, 1, gx_count) for a in first_parts],
        [cut(a, 1, gx_count) for a in second_parts],
        gx_count,
    )
    second_parts = exchange(second_parts, "gx", 1)
    first_parts = exchange(first_parts, "gx", 1)
    first_total = sum(a.astype(F32) for a in first_parts)
    second_total = sum(a.astype(F32) for a in second_parts)
    return (
        first_total.reshape(own_rows, hid),
        second_total.reshape(own_rows, feat),
        loss.reshape(1),
    )


def solution(mesh):
    return jax.shard_map(
        on_device,
        mesh=mesh,
        in_specs=(
            P(("gx", "gy"), None),
            P(),
            P(),
            P(("gx", "gy")),
            P(("gx", "gy")),
            P(("gx", "gy"), None),
        ),
        out_specs=(P(("gx", "gy"), None), P(("gx", "gy"), None), P(("gx", "gy"))),
        check_vma=False,
    )
```

```python
import functools

import jax
import jax.numpy as jnp
from jax import lax
from jax.experimental import pallas as pl
from jax.experimental.pallas import tpu as pltpu
from jax.sharding import PartitionSpec as P

CAP = 512
POWERS = 16
BF16 = jnp.bfloat16
F32 = jnp.float32
EXACT = lax.Precision.HIGHEST
VMEM = pl.BlockSpec(memory_space=pltpu.VMEM)
SMEM = pl.BlockSpec(memory_space=pltpu.SMEM)
ANY = pl.BlockSpec(memory_space=pl.ANY)
PARAMS = pltpu.CompilerParams(vmem_limit_bytes=24 * 1024 * 1024)


def cost(work):
    return pl.CostEstimate(flops=int(work), bytes_accessed=0, transcendentals=0)


def dot(left, right, left_dim=1, right_dim=0, precision=None):
    return lax.dot_general(
        left,
        right,
        (((left_dim,), (right_dim,)), ((), ())),
        preferred_element_type=F32,
        precision=precision,
    )


def iota(shape, dim):
    return lax.broadcasted_iota(jnp.int32, shape, dim)


def dispatch_kernel(devices, assign_hbm, targ_hbm, rows_hbm, out_ref, assign_ref, targ_ref, rows_ref, sems):
    copies = [
        pltpu.make_async_copy(source, target, sems.at[i])
        for i, (source, target) in enumerate(
            ((assign_hbm, assign_ref), (targ_hbm, targ_ref), (rows_hbm, rows_ref))
        )
    ]
    for copy in copies:
        copy.start()
    copies[0].wait()
    assign = assign_ref[...]
    count, width = rows_ref.shape
    per_slot = CAP // devices
    onehot = iota((devices, count), 0) == assign
    earlier = (iota((count, count), 0) < iota((count, count), 1)).astype(BF16)
    rank = dot(onehot.astype(BF16), earlier)
    slot = jnp.sum(jnp.where(onehot, rank, 0.0), axis=0, keepdims=True)
    place = assign * per_slot + slot.astype(jnp.int32)
    here = iota((CAP, count), 0) == place
    copies[1].wait()
    targ = targ_ref[...].astype(F32).reshape(1, count)
    targ = jnp.sum(jnp.where(here, targ, 0.0), axis=1, keepdims=True)
    copies[2].wait()
    placed = dot(here.astype(BF16), rows_ref[...]).astype(BF16)
    if tight(devices):
        for i in range(width // 128):
            block = placed[:, i * 128 : (i + 1) * 128].reshape(devices, per_slot, 128)
            out_ref[:, i * per_slot : (i + 1) * per_slot, :] = block
        targ = targ.reshape(devices, per_slot, 1)
        lane = iota((devices, per_slot // 2, 128), 2)
        targ = jnp.where(lane < 64, targ[:, : per_slot // 2], targ[:, per_slot // 2 :])
        out_ref[:, width // 128 * per_slot :, :] = targ.astype(BF16)
    else:
        out_ref[:, :width] = placed
        out_ref[:, width:] = jnp.broadcast_to(targ, (CAP, 128)).astype(BF16)


def tight(devices):
    return (CAP // devices) % 16 == 0


def gram_rows_to_column(gram, row):
    parts = []
    for start in range(0, CAP, 64):
        product = gram[start : start + 64, :] * row
        folded = sum(product[:, lane : lane + 128] for lane in range(0, CAP, 128))
        parts.append(jnp.sum(folded, axis=1, keepdims=True))
    return jnp.concatenate(parts, axis=0)


def gram_column_to_row(gram, column):
    total = jnp.zeros((8, CAP), F32)
    for start in range(0, CAP, 64):
        product = gram[start : start + 64, :] * column[start : start + 64, :]
        total = total + jnp.sum(product.reshape(8, 8, CAP), axis=0)
    return jnp.sum(total, axis=0, keepdims=True)


def fit_kernel(
    blocks,
    noise_ref,
    got_ref,
    first_ref,
    second_hbm,
    pre_ref,
    grad_ref,
    xt_ref,
    ht_ref,
    loss_ref,
    hid_ref,
    feat_ref,
    gram_ref,
    x_ref,
    targ_ref,
    second_ref,
    sem,
):
    din, hid = first_ref.shape
    feat = second_hbm.shape[1]
    step = 128
    chunks = CAP // step
    second_copy = pltpu.make_async_copy(second_hbm, second_ref, sem)
    second_copy.start()
    if tight(blocks):
        per_slot = CAP // blocks
        for i in range(din // 128):
            block = got_ref[:, i * per_slot : (i + 1) * per_slot, :]
            x_ref[:, i * 128 : (i + 1) * 128] = block.reshape(CAP, 128)
        packed = got_ref[:, din // 128 * per_slot :, :].astype(F32)
        lanes = (blocks, per_slot // 2, 128)
        parts = [jnp.broadcast_to(packed[:, :, i : i + 1], lanes) for i in (0, 64)]
        targ_ref[...] = jnp.concatenate(parts, axis=1).reshape(CAP, 128)
    else:
        x_ref[...] = got_ref[:, :din]
        targ_ref[...] = got_ref[:, din:].astype(F32)

    def split_parity(source, target):
        turned = source.T.reshape(blocks // 2, 2, din // blocks, CAP)
        target[0] = turned[:, 0].reshape(din // 2, CAP)
        target[1] = turned[:, 1].reshape(din // 2, CAP)

    @pl.loop(0, chunks)
    def _(i):
        rows = pl.ds(pl.multiple_of(i * step, step), step)
        pre = dot(x_ref[rows, :], first_ref[...])
        pre_ref[rows, :] = pre
        hid_ref[rows, :] = (pre * jax.nn.sigmoid(pre)).astype(BF16)

    second_copy.wait()

    @pl.loop(0, chunks)
    def _(i):
        rows = pl.ds(pl.multiple_of(i * step, step), step)
        feat_ref[rows, :] = dot(hid_ref[rows, :], second_ref[...]).astype(BF16)

    split_parity(x_ref[...], xt_ref)
    split_parity(hid_ref[...], ht_ref)

    feats = feat_ref[...]
    gram_ref[...] = dot(feats, feats, 1, 1) * (1.0 / feat)
    gram = gram_ref[...]
    noise = noise_ref[0]
    squares = sum(
        jnp.sum((gram[i : i + 64, :] * gram[i : i + 64, :]).reshape(8, 8, CAP), axis=0)
        for i in range(0, CAP, 64)
    )
    root = jnp.sqrt(jnp.sum(squares, keepdims=True) + 1e-06)
    theta = root + noise
    inverse = 1.0 / theta
    shrink = root * inverse

    targ = targ_ref[...]
    column = targ[:, :1]
    lane = iota((CAP, 128), 1)
    sub = iota((POWERS, CAP), 0)
    columns = jnp.where(lane == 0, targ, 0.0)
    row_set = jnp.zeros((POWERS, CAP), F32)
    targ_row = targ.T[:1, :]
    row = None
    for k in range(1, POWERS - 1):
        if k % 2 == 1:
            before = targ_row if k == 1 else columns.T[k - 1 : k, :]
            row = shrink * before - gram_column_to_row(gram, column) * inverse
            row_set = row_set + jnp.where(sub == k, row, 0.0)
        else:
            before = row.T
            column = shrink * before - gram_rows_to_column(gram, row) * inverse
            columns = columns + jnp.where(lane == k, column, 0.0)
    powers = row_set + columns.T[:POWERS, :]
    moments = jnp.sum(powers * targ_row, axis=1, keepdims=True)
    last = jnp.sum(powers[7:8, :] * powers[8:9, :], axis=1, keepdims=True)
    loss_ref[...] = 0.5 * inverse * (jnp.sum(moments, axis=0, keepdims=True) + last)
    mask = (iota((POWERS, POWERS), 0) + iota((POWERS, POWERS), 1) <= POWERS - 2).astype(F32)
    sums = dot(mask, powers, precision=EXACT)
    outer = dot(powers, sums, 0, 0, precision=EXACT) + (16.0 * last / root) * gram
    high = outer.astype(BF16)
    low = (outer - high.astype(F32)).astype(BF16)
    scale = -inverse * inverse * (1.0 / feat)
    grad_ref[...] = ((dot(high, feats) + dot(low, feats)) * scale).astype(BF16)


def second_kernel(parity_ref, grad_ref, ht_ref, keep_ref, send_ref):
    parity = parity_ref[0]
    keep_ref[...] = dot(ht_ref[parity], grad_ref[...])
    send_ref[...] = dot(ht_ref[1 - parity], grad_ref[...])


def first_kernel(parity_ref, grad_ref, second_ref, pre_ref, xt_ref, keep_ref, send_ref, pgrad_ref):
    step = 128
    parity = parity_ref[0]

    @pl.loop(0, CAP // step)
    def _(i):
        rows = pl.ds(pl.multiple_of(i * step, step), step)
        hidden_grad = dot(grad_ref[rows, :], second_ref[...], 1, 1)
        pre = pre_ref[rows, :]
        sigma = jax.nn.sigmoid(pre)
        pgrad_ref[rows, :] = (hidden_grad * sigma * (1.0 + pre * (1.0 - sigma))).astype(BF16)

    send_ref[...] = dot(xt_ref[1 - parity], pgrad_ref[...])
    keep_ref[...] = dot(xt_ref[parity], pgrad_ref[...])


def split_kernel(group, leading, place_ref, *refs):
    parts, outs = refs[:-group], refs[-group:]
    place = place_ref[0]
    for d, out in enumerate(outs):
        target = jnp.bitwise_xor(place, d)
        index = (target,) if leading else (slice(None), target)
        total = parts[0][index].astype(F32)
        for part in parts[1:]:
            total = total + part[index].astype(F32)
        out[...] = total.astype(out.dtype)


def split_stage(place, parts, outer, group, own_rows, leading=False):
    columns = parts[0].shape[-1]
    shape = (*((group, outer) if leading else (outer, group)), own_rows, columns)
    made = (outer, own_rows, columns)
    return pl.pallas_call(
        functools.partial(split_kernel, group, leading),
        out_shape=[jax.ShapeDtypeStruct(made, F32 if d == 0 else BF16) for d in range(group)],
        in_specs=[SMEM] + [VMEM] * len(parts),
        out_specs=[VMEM] * group,
        cost_estimate=cost(outer * group * own_rows * columns * 1000),
        compiler_params=PARAMS,
    )(place, *[part.reshape(shape) for part in parts])


def swap(array, axis, distance):
    count = lax.axis_size(axis)
    return lax.ppermute(array, axis, [(i, i ^ distance) for i in range(count)])


def exchange(parts, axis, unit):
    return [parts[0]] + [swap(parts[d], axis, d * unit) for d in range(1, len(parts))]


def on_device(inputs, first_weight, second_weight, targets, noise_var, assignment):
    gx_count = lax.axis_size("gx")
    gy_count = lax.axis_size("gy")
    devices = gx_count * gy_count
    per_slot = CAP // devices
    rows, din = inputs.shape
    hid, feat = second_weight.shape
    own_rows = din // devices
    gx = lax.axis_index("gx")
    gy = lax.axis_index("gy")

    def scalar(x):
        return x.astype(jnp.int32).reshape(1)

    if tight(devices):
        sent_shape = packed_shape = (devices, din // 128 * per_slot + per_slot // 2, 128)
    else:
        sent_shape, packed_shape = (CAP, din + 128), (devices, per_slot, din + 128)
    sent = pl.pallas_call(
        functools.partial(dispatch_kernel, devices),
        out_shape=jax.ShapeDtypeStruct(sent_shape, BF16),
        in_specs=[ANY] * 3,
        out_specs=VMEM,
        scratch_shapes=[
            pltpu.VMEM((1, rows), jnp.int32),
            pltpu.VMEM((rows,), BF16),
            pltpu.VMEM((rows, din), BF16),
            pltpu.SemaphoreType.DMA((3,)),
        ],
        cost_estimate=cost(2 * CAP * rows * din),
        compiler_params=PARAMS,
    )(assignment.reshape(1, rows), targets, inputs)
    got = lax.all_to_all(
        sent.reshape(packed_shape), ("gx", "gy"), split_axis=0, concat_axis=0, tiled=True
    ).reshape(sent_shape)

    half = din // 2
    pre, grad, xt, ht, loss = pl.pallas_call(
        functools.partial(fit_kernel, devices),
        out_shape=[
            jax.ShapeDtypeStruct((CAP, hid), F32),
            jax.ShapeDtypeStruct((CAP, feat), BF16),
            jax.ShapeDtypeStruct((2, half, CAP), BF16),
            jax.ShapeDtypeStruct((2, half, CAP), BF16),
            jax.ShapeDtypeStruct((1, 1), F32),
        ],
        in_specs=[SMEM, VMEM, VMEM, ANY],
        out_specs=[VMEM] * 5,
        scratch_shapes=[
            pltpu.VMEM((CAP, hid), BF16),
            pltpu.VMEM((CAP, feat), BF16),
            pltpu.VMEM((CAP, CAP), F32),
            pltpu.VMEM((CAP, din), BF16),
            pltpu.VMEM((CAP, 128), F32),
            pltpu.VMEM((hid, feat), BF16),
            pltpu.SemaphoreType.DMA,
        ],
        cost_estimate=cost(8 * CAP * din * hid),
        compiler_params=PARAMS,
    )(noise_var, got, first_weight, second_weight)

    parity = scalar(gy % 2)
    keep2, send2 = pl.pallas_call(
        second_kernel,
        out_shape=[jax.ShapeDtypeStruct((half, feat), F32)] * 2,
        in_specs=[SMEM, VMEM, VMEM],
        out_specs=[VMEM] * 2,
        cost_estimate=cost(2 * CAP * hid * feat * 2),
        compiler_params=PARAMS,
    )(parity, grad, ht)
    pre, keep2, send2 = lax.optimization_barrier((pre, keep2, send2))
    keep1, send1 = pl.pallas_call(
        first_kernel,
        out_shape=[jax.ShapeDtypeStruct((half, hid), F32)] * 2,
        in_specs=[SMEM, VMEM, VMEM, VMEM, VMEM],
        out_specs=[VMEM] * 2,
        scratch_shapes=[pltpu.VMEM((CAP, hid), BF16)],
        cost_estimate=cost(2 * CAP * din * hid * 4),
        compiler_params=PARAMS,
    )(parity, grad, second_weight, pre, xt)

    plane = gy_count // 2

    def over_gy(parts, outer):
        return exchange(split_stage(scalar(gy // 2), parts, outer, plane, own_rows), "gy", 2)

    def over_gx(parts, outer):
        return exchange(split_stage(scalar(gx), parts, outer, gx_count, own_rows, True), "gx", 1)

    def added(parts):
        return sum(part.astype(F32) for part in parts).reshape(own_rows, -1)

    second_parts = [keep2, swap(send2, "gy", 1)]
    send1, second_parts[1] = lax.optimization_barrier((send1, second_parts[1]))
    first_parts = [keep1, swap(send1, "gy", 1)]
    second_parts[0], first_parts[0] = lax.optimization_barrier((second_parts[0], first_parts[0]))
    second_parts = over_gx(second_parts, plane)
    first_parts = over_gy(first_parts, gx_count)
    second_parts = over_gy(second_parts, 1)
    first_parts = over_gx(first_parts, 1)
    second_total = added(second_parts)
    first_total = added(first_parts)
    return (first_total, second_total, loss.reshape(1))


def solution(mesh):
    return jax.shard_map(
        on_device,
        mesh=mesh,
        in_specs=(
            P(("gx", "gy"), None),
            P(),
            P(),
            P(("gx", "gy")),
            P(("gx", "gy")),
            P(("gx", "gy"), None),
        ),
        out_specs=(P(("gx", "gy"), None), P(("gx", "gy"), None), P(("gx", "gy"))),
        check_vma=False,
    )
```

```python
import functools

import jax
import jax.numpy as jnp
from jax import lax
from jax.experimental import pallas as pl
from jax.experimental.pallas import tpu as pltpu
from jax.sharding import PartitionSpec as P

CAP = 512
POWERS = 16
BF16 = jnp.bfloat16
F32 = jnp.float32
EXACT = lax.Precision.HIGHEST
VMEM = pl.BlockSpec(memory_space=pltpu.VMEM)
SMEM = pl.BlockSpec(memory_space=pltpu.SMEM)
HBM = pl.BlockSpec(memory_space=pltpu.HBM)
PARAMS = pltpu.CompilerParams(vmem_limit_bytes=24 * 1024 * 1024)


def cost(work):
    return pl.CostEstimate(flops=int(work), bytes_accessed=0, transcendentals=0)


def dot(left, right, left_dim=1, right_dim=0, precision=None):
    return lax.dot_general(
        left,
        right,
        (((left_dim,), (right_dim,)), ((), ())),
        preferred_element_type=F32,
        precision=precision,
    )


def iota(shape, dim):
    return lax.broadcasted_iota(jnp.int32, shape, dim)


def dispatch_kernel(devices, assign_hbm, targ_hbm, rows_hbm, out_ref, assign_ref, targ_ref, rows_ref, sems):
    copies = [
        pltpu.make_async_copy(source, target, sems.at[i])
        for i, (source, target) in enumerate(
            ((assign_hbm, assign_ref), (targ_hbm, targ_ref), (rows_hbm, rows_ref))
        )
    ]
    for copy in copies:
        copy.start()
    copies[0].wait()
    assign = assign_ref[...]
    count, width = rows_ref.shape
    per_slot = CAP // devices
    onehot = iota((devices, count), 0) == assign
    earlier = (iota((count, count), 0) < iota((count, count), 1)).astype(BF16)
    rank = dot(onehot.astype(BF16), earlier)
    slot = jnp.sum(jnp.where(onehot, rank, 0.0), axis=0, keepdims=True)
    place = assign * per_slot + slot.astype(jnp.int32)
    here = iota((CAP, count), 0) == place
    copies[1].wait()
    targ = targ_ref[...].astype(F32).reshape(1, count)
    targ = jnp.sum(jnp.where(here, targ, 0.0), axis=1, keepdims=True)
    copies[2].wait()
    placed = dot(here.astype(BF16), rows_ref[...]).astype(BF16)
    if tight(devices):
        for i in range(width // 128):
            block = placed[:, i * 128 : (i + 1) * 128].reshape(devices, per_slot, 128)
            out_ref[:, i * per_slot : (i + 1) * per_slot, :] = block
        targ = targ.reshape(devices, per_slot, 1)
        lane = iota((devices, per_slot // 2, 128), 2)
        targ = jnp.where(lane < 64, targ[:, : per_slot // 2], targ[:, per_slot // 2 :])
        out_ref[:, width // 128 * per_slot :, :] = targ.astype(BF16)
    else:
        out_ref[:, :width] = placed
        out_ref[:, width:] = jnp.broadcast_to(targ, (CAP, 128)).astype(BF16)


def tight(devices):
    return (CAP // devices) % 16 == 0


def unpack_kernel(devices, got_ref, x_ref, targ_ref, xt_ref):
    din = x_ref.shape[1]
    if tight(devices):
        per_slot = CAP // devices
        for i in range(din // 128):
            block = got_ref[:, i * per_slot : (i + 1) * per_slot, :]
            x_ref[:, i * 128 : (i + 1) * 128] = block.reshape(CAP, 128)
        packed = got_ref[:, din // 128 * per_slot :, :].astype(F32)
        lanes = (devices, per_slot // 2, 128)
        parts = [jnp.broadcast_to(packed[:, :, i : i + 1], lanes) for i in (0, 64)]
        targ_ref[...] = jnp.concatenate(parts, axis=1).reshape(CAP, 128)
    else:
        x_ref[...] = got_ref[:, :din]
        targ_ref[...] = got_ref[:, din:].astype(F32)
    split_parity(devices, x_ref[...], xt_ref)


def split_parity(blocks, source, target):
    width = source.shape[1]
    turned = source.T.reshape(blocks // 2, 2, width // blocks, CAP)
    target[0] = turned[:, 0].reshape(width // 2, CAP)
    target[1] = turned[:, 1].reshape(width // 2, CAP)


def row_to_column(gram, row):
    parts = []
    for start in range(0, CAP, 64):
        product = gram[start : start + 64, :] * row
        folded = sum(product[:, lane : lane + 128] for lane in range(0, CAP, 128))
        parts.append(jnp.sum(folded, axis=1, keepdims=True))
    return jnp.concatenate(parts, axis=0)


def column_to_row(gram, column):
    total = jnp.zeros((8, CAP), F32)
    for start in range(0, CAP, 64):
        product = gram[start : start + 64, :] * column[start : start + 64, :]
        total = total + jnp.sum(product.reshape(8, 8, CAP), axis=0)
    return jnp.sum(total, axis=0, keepdims=True)


def fit_kernel(
    blocks,
    noise_ref,
    x_ref,
    targ_ref,
    first_ref,
    second_ref,
    pre_ref,
    grad_ref,
    ht_ref,
    loss_ref,
    hid_ref,
    feat_ref,
    gram_ref,
    resid_ref,
):
    hid = first_ref.shape[1]
    feat = second_ref.shape[1]
    step = 256
    for i in range(0, hid, step):
        pre = dot(x_ref[...], first_ref[:, i : i + step])
        pre_ref[:, i : i + step] = pre
        hid_ref[:, i : i + step] = (pre * jax.nn.sigmoid(pre)).astype(BF16)
    for i in range(0, feat, step):
        feat_ref[:, i : i + step] = dot(hid_ref[...], second_ref[:, i : i + step]).astype(BF16)
    split_parity(blocks, hid_ref[...], ht_ref)

    feats = feat_ref[...]
    gram_ref[...] = dot(feats, feats, 1, 1) * (1.0 / feat)
    gram = gram_ref[...]
    noise = noise_ref[0]
    squares = sum(
        jnp.sum((gram[i : i + 64, :] * gram[i : i + 64, :]).reshape(8, 8, CAP), axis=0)
        for i in range(0, CAP, 64)
    )
    root = jnp.sqrt(jnp.sum(squares, keepdims=True) + 1e-06)
    theta = root + noise
    inverse = 1.0 / theta
    diagonal = iota((CAP, CAP), 0) == iota((CAP, CAP), 1)
    resid_ref[...] = (jnp.where(diagonal, root, 0.0) - gram) * inverse
    resid = resid_ref

    targ = targ_ref[...]
    column = targ[:, :1]
    lane = iota((CAP, 128), 1)
    sub = iota((POWERS, CAP), 0)
    columns = jnp.where(lane == 0, targ, 0.0)
    row_set = jnp.zeros((POWERS, CAP), F32)
    targ_row = targ.T[:1, :]
    for k in range(1, POWERS - 1):
        if k % 2 == 1:
            row = column_to_row(resid, column)
            row_set = row_set + jnp.where(sub == k, row, 0.0)
        else:
            column = row_to_column(resid, row)
            columns = columns + jnp.where(lane == k, column, 0.0)
    powers = row_set + columns.T[:POWERS, :]
    moments = jnp.sum(powers * targ_row, axis=1, keepdims=True)
    last = jnp.sum(powers[7:8, :] * powers[8:9, :], axis=1, keepdims=True)
    loss_ref[...] = 0.5 * inverse * (jnp.sum(moments, axis=0, keepdims=True) + last)
    mask = (iota((POWERS, POWERS), 0) + iota((POWERS, POWERS), 1) <= POWERS - 2).astype(F32)
    sums = dot(mask, powers, precision=EXACT)
    outer = dot(powers, sums, 0, 0, precision=EXACT) + (16.0 * last / root) * gram
    high = outer.astype(BF16)
    low = (outer - high.astype(F32)).astype(BF16)
    scale = -inverse * inverse * (1.0 / feat)
    grad_ref[...] = ((dot(high, feats) + dot(low, feats)) * scale).astype(BF16)


def second_kernel(grad_ref, ht_ref, keep_ref, send_ref):
    parity = lax.axis_index("gy") % 2
    keep_ref[...] = dot(ht_ref[parity], grad_ref[...])
    send_ref[...] = dot(ht_ref[1 - parity], grad_ref[...]).astype(BF16)


def first_kernel(grad_ref, second_ref, pre_ref, xt_ref, keep_ref, send_ref):
    step = 256
    parity = lax.axis_index("gy") % 2
    for i in range(0, pre_ref.shape[1], step):
        hidden_grad = dot(grad_ref[...], second_ref[i : i + step, :], 1, 1)
        pre = pre_ref[:, i : i + step]
        sigma = jax.nn.sigmoid(pre)
        pre_grad = (hidden_grad * sigma * (1.0 + pre * (1.0 - sigma))).astype(BF16)
        send_ref[:, i : i + step] = dot(xt_ref[1 - parity], pre_grad).astype(BF16)
        keep_ref[:, i : i + step] = dot(xt_ref[parity], pre_grad)


def split_kernel(group, leading, axis, unit, *refs):
    parts, outs = refs[:-group], refs[-group:]
    place = lax.axis_index(axis) // unit
    for d, out in enumerate(outs):
        target = jnp.bitwise_xor(place, d)
        index = (target,) if leading else (slice(None), target)
        total = parts[0][index].astype(F32)
        for part in parts[1:]:
            total = total + part[index].astype(F32)
        out[...] = total.astype(out.dtype)


def split_stage(axis, unit, parts, outer, group, own_rows, leading=False):
    columns = parts[0].shape[-1]
    shape = (*((group, outer) if leading else (outer, group)), own_rows, columns)
    made = (outer, own_rows, columns)
    return pl.pallas_call(
        functools.partial(split_kernel, group, leading, axis, unit),
        out_shape=[jax.ShapeDtypeStruct(made, F32 if d == 0 else BF16) for d in range(group)],
        in_specs=[VMEM] * len(parts),
        out_specs=[VMEM] * group,
        cost_estimate=cost(outer * group * own_rows * columns * 1000),
        compiler_params=PARAMS,
    )(*[part.reshape(shape) for part in parts])


def swap(array, axis, distance):
    count = lax.axis_size(axis)
    return lax.ppermute(array, axis, [(i, i ^ distance) for i in range(count)])


def exchange(parts, axis, unit):
    return [parts[0]] + [swap(parts[d], axis, d * unit) for d in range(1, len(parts))]


def on_device(inputs, first_weight, second_weight, targets, noise_var, assignment):
    gx_count = lax.axis_size("gx")
    gy_count = lax.axis_size("gy")
    devices = gx_count * gy_count
    per_slot = CAP // devices
    rows, din = inputs.shape
    hid, feat = second_weight.shape
    own_rows = din // devices
    if tight(devices):
        sent_shape = packed_shape = (devices, din // 128 * per_slot + per_slot // 2, 128)
    else:
        sent_shape, packed_shape = (CAP, din + 128), (devices, per_slot, din + 128)
    sent = pl.pallas_call(
        functools.partial(dispatch_kernel, devices),
        out_shape=jax.ShapeDtypeStruct(sent_shape, BF16),
        in_specs=[HBM] * 3,
        out_specs=VMEM,
        scratch_shapes=[
            pltpu.VMEM((1, rows), jnp.int32),
            pltpu.VMEM((rows,), BF16),
            pltpu.VMEM((rows, din), BF16),
            pltpu.SemaphoreType.DMA((3,)),
        ],
        cost_estimate=cost(2 * CAP * rows * din),
    )(assignment.reshape(1, rows), targets, inputs)
    got = lax.all_to_all(
        sent.reshape(packed_shape), ("gx", "gy"), split_axis=0, concat_axis=0, tiled=True
    ).reshape(sent_shape)

    half = din // 2
    x, targ, xt = pl.pallas_call(
        functools.partial(unpack_kernel, devices),
        out_shape=[
            jax.ShapeDtypeStruct((CAP, din), BF16),
            jax.ShapeDtypeStruct((CAP, 128), F32),
            jax.ShapeDtypeStruct((2, half, CAP), BF16),
        ],
        in_specs=[VMEM],
        out_specs=[VMEM] * 3,
        cost_estimate=cost(2 * CAP * din * hid),
        compiler_params=PARAMS,
    )(got)
    pre, grad, ht, loss = pl.pallas_call(
        functools.partial(fit_kernel, devices),
        out_shape=[
            jax.ShapeDtypeStruct((CAP, hid), F32),
            jax.ShapeDtypeStruct((CAP, feat), BF16),
            jax.ShapeDtypeStruct((2, hid // 2, CAP), BF16),
            jax.ShapeDtypeStruct((1, 1), F32),
        ],
        in_specs=[SMEM] + [VMEM] * 4,
        out_specs=[VMEM] * 4,
        scratch_shapes=[
            pltpu.VMEM((CAP, hid), BF16),
            pltpu.VMEM((CAP, feat), BF16),
            pltpu.VMEM((CAP, CAP), F32),
            pltpu.VMEM((CAP, CAP), F32),
        ],
        cost_estimate=cost(8 * CAP * din * hid),
        compiler_params=PARAMS,
    )(noise_var, x, targ, first_weight, second_weight)

    keep1, send1 = pl.pallas_call(
        first_kernel,
        out_shape=[jax.ShapeDtypeStruct((half, hid), kind) for kind in (F32, BF16)],
        in_specs=[VMEM] * 4,
        out_specs=[VMEM] * 2,
        cost_estimate=cost(2 * CAP * din * hid * 4),
        compiler_params=PARAMS,
    )(grad, second_weight, pre, xt)
    keep1, ht = lax.optimization_barrier((keep1, ht))
    keep2, send2 = pl.pallas_call(
        second_kernel,
        out_shape=[jax.ShapeDtypeStruct((hid // 2, feat), kind) for kind in (F32, BF16)],
        in_specs=[VMEM] * 2,
        out_specs=[VMEM] * 2,
        cost_estimate=cost(2 * CAP * hid * feat * 2),
        compiler_params=PARAMS,
    )(grad, ht)

    plane = gy_count // 2

    def by_gy(parts, outer):
        return split_stage("gy", 2, parts, outer, plane, own_rows)

    def by_gx(parts, outer):
        return split_stage("gx", 1, parts, outer, gx_count, own_rows, True)

    def added(parts):
        return sum(part.astype(F32) for part in parts).reshape(own_rows, -1)

    first_parts = [*by_gy([keep1, swap(send1, "gy", 1)], gx_count)]
    first_parts[0], keep2 = lax.optimization_barrier((first_parts[0], keep2))
    first_parts = exchange(first_parts, "gy", 2)
    second_parts = exchange(by_gx([keep2, swap(send2, "gy", 1)], plane), "gx", 1)
    first_parts = exchange(by_gx(first_parts, 1), "gx", 1)
    first_parts[1], second_parts[0] = lax.optimization_barrier((first_parts[1], second_parts[0]))
    second_parts = exchange(by_gy(second_parts, 1), "gy", 2)
    second_total = added(second_parts)
    first_total = added(first_parts)
    return (first_total, second_total, loss.reshape(1))


def solution(mesh):
    return jax.shard_map(
        on_device,
        mesh=mesh,
        in_specs=(
            P(("gx", "gy"), None),
            P(),
            P(),
            P(("gx", "gy")),
            P(("gx", "gy")),
            P(("gx", "gy"), None),
        ),
        out_specs=(P(("gx", "gy"), None), P(("gx", "gy"), None), P(("gx", "gy"))),
        check_vma=False,
    )
```

```python
import functools

import jax
import jax.numpy as jnp
from jax import lax
from jax.experimental import pallas as pl
from jax.experimental.pallas import tpu as pltpu
from jax.sharding import PartitionSpec as P

CAP = 512
POWERS = 16
BF16 = jnp.bfloat16
F32 = jnp.float32
VMEM = pl.BlockSpec(memory_space=pltpu.VMEM)
SMEM = pl.BlockSpec(memory_space=pltpu.SMEM)
HBM = pl.BlockSpec(memory_space=pltpu.HBM)
PARAMS = pltpu.CompilerParams(vmem_limit_bytes=24 * 1024 * 1024)


def cost(work):
    return pl.CostEstimate(flops=int(work), bytes_accessed=0, transcendentals=0)


def dot(left, right, left_dim=1, right_dim=0):
    return lax.dot_general(
        left,
        right,
        (((left_dim,), (right_dim,)), ((), ())),
        preferred_element_type=F32,
    )


def iota(shape, dim):
    return lax.broadcasted_iota(jnp.int32, shape, dim)


def dispatch_kernel(devices, assign_hbm, targ_hbm, rows_hbm, out_ref, assign_ref, targ_ref, rows_ref, sems):
    copies = [
        pltpu.make_async_copy(source, target, sems.at[i])
        for i, (source, target) in enumerate(
            ((assign_hbm, assign_ref), (targ_hbm, targ_ref), (rows_hbm, rows_ref))
        )
    ]
    for copy in copies:
        copy.start()
    copies[0].wait()
    assign = assign_ref[...]
    count, width = rows_ref.shape
    per_slot = CAP // devices
    onehot = iota((devices, count), 0) == assign
    earlier = (iota((count, count), 0) < iota((count, count), 1)).astype(BF16)
    rank = dot(onehot.astype(BF16), earlier)
    slot = jnp.sum(jnp.where(onehot, rank, 0.0), axis=0, keepdims=True)
    place = assign * per_slot + slot.astype(jnp.int32)
    here = iota((CAP, count), 0) == place
    copies[1].wait()
    targ = targ_ref[...].astype(F32).reshape(1, count)
    targ = jnp.sum(jnp.where(here, targ, 0.0), axis=1, keepdims=True)
    copies[2].wait()
    placed = dot(here.astype(BF16), rows_ref[...]).astype(BF16)
    if tight(devices):
        for i in range(width // 128):
            block = placed[:, i * 128 : (i + 1) * 128].reshape(devices, per_slot, 128)
            out_ref[:, i * per_slot : (i + 1) * per_slot, :] = block
        targ = targ.reshape(devices, per_slot, 1)
        lane = iota((devices, per_slot // 2, 128), 2)
        targ = jnp.where(lane < 64, targ[:, : per_slot // 2], targ[:, per_slot // 2 :])
        out_ref[:, width // 128 * per_slot :, :] = targ.astype(BF16)
    else:
        out_ref[:, :width] = placed
        out_ref[:, width:] = jnp.broadcast_to(targ, (CAP, 128)).astype(BF16)


def tight(devices):
    return (CAP // devices) % 16 == 0


def unpack_kernel(devices, got_ref, x_ref, targ_ref, xt_ref):
    din = x_ref.shape[1]
    if tight(devices):
        per_slot = CAP // devices
        for i in range(din // 128):
            block = got_ref[:, i * per_slot : (i + 1) * per_slot, :]
            x_ref[:, i * 128 : (i + 1) * 128] = block.reshape(CAP, 128)
        packed = got_ref[:, din // 128 * per_slot :, :].astype(F32)
        lanes = (devices, per_slot // 2, 128)
        parts = [jnp.broadcast_to(packed[:, :, i : i + 1], lanes) for i in (0, 64)]
        targ_ref[...] = jnp.concatenate(parts, axis=1).reshape(CAP, 128)
    else:
        x_ref[...] = got_ref[:, :din]
        targ_ref[...] = got_ref[:, din:].astype(F32)
    split_parity(devices, x_ref[...], xt_ref)


def split_parity(blocks, source, target):
    width = source.shape[1]
    turned = source.T.reshape(blocks // 2, 2, width // blocks, CAP)
    target[0] = turned[:, 0].reshape(width // 2, CAP)
    target[1] = turned[:, 1].reshape(width // 2, CAP)


def pieces(array, count):
    made = []
    for _ in range(count):
        made.append(array.astype(BF16))
        array = array - made[-1].astype(F32)
    return made


def row_to_column(gram, row):
    parts = []
    for start in range(0, CAP, 64):
        product = gram[start : start + 64, :] * row
        folded = sum(product[:, lane : lane + 128] for lane in range(0, CAP, 128))
        parts.append(jnp.sum(folded, axis=1, keepdims=True))
    return jnp.concatenate(parts, axis=0)


def column_to_row(gram, column):
    total = jnp.zeros((8, CAP), F32)
    for start in range(0, CAP, 64):
        product = gram[start : start + 64, :] * column[start : start + 64, :]
        total = total + jnp.sum(product.reshape(8, 8, CAP), axis=0)
    return jnp.sum(total, axis=0, keepdims=True)


def hidden_kernel(x_ref, first_ref, pre_ref, hid_ref):
    step = 256
    for i in range(0, first_ref.shape[1], step):
        pre = dot(x_ref[...], first_ref[:, i : i + step])
        pre_ref[:, i : i + step] = pre
        hid_ref[:, i : i + step] = (pre * jax.nn.sigmoid(pre)).astype(BF16)


def fit_kernel(noise_ref, hid_ref, targ_ref, second_ref, grad_ref, loss_ref, feat_ref, gram_ref, resid_ref):
    feat = second_ref.shape[1]
    step = 256
    for i in range(0, feat, step):
        feat_ref[:, i : i + step] = dot(hid_ref[...], second_ref[:, i : i + step]).astype(BF16)

    feats = feat_ref[...]
    gram_ref[...] = dot(feats, feats, 1, 1) * (1.0 / feat)
    gram = gram_ref[...]
    noise = noise_ref[0]
    squares = sum(
        jnp.sum((gram[i : i + 64, :] * gram[i : i + 64, :]).reshape(8, 8, CAP), axis=0)
        for i in range(0, CAP, 64)
    )
    root = jnp.sqrt(jnp.sum(squares, keepdims=True) + 1e-06)
    theta = root + noise
    inverse = 1.0 / theta
    diagonal = iota((CAP, CAP), 0) == iota((CAP, CAP), 1)
    resid_ref[...] = (jnp.where(diagonal, root, 0.0) - gram) * inverse
    resid = resid_ref

    targ = targ_ref[...]
    column = targ[:, :1]
    lane = iota((CAP, 128), 1)
    sub = iota((POWERS, CAP), 0)
    columns = jnp.where(lane == 0, targ, 0.0)
    row_set = jnp.zeros((POWERS, CAP), F32)
    targ_row = targ.T[:1, :]
    for k in range(1, POWERS - 1):
        if k % 2 == 1:
            row = column_to_row(resid, column)
            row_set = row_set + jnp.where(sub == k, row, 0.0)
        else:
            column = row_to_column(resid, row)
            columns = columns + jnp.where(lane == k, column, 0.0)
    powers = row_set + columns.T[:POWERS, :]
    moments = jnp.sum(powers * targ_row, axis=1, keepdims=True)
    last = jnp.sum(powers[7:8, :] * powers[8:9, :], axis=1, keepdims=True)
    loss_ref[...] = 0.5 * inverse * (jnp.sum(moments, axis=0, keepdims=True) + last)
    mask = (iota((POWERS, POWERS), 0) + iota((POWERS, POWERS), 1) <= POWERS - 2).astype(BF16)
    top, middle, bottom = pieces(powers, 3)
    stacked = jnp.concatenate([top, middle, bottom], axis=0)
    sums = dot(jnp.concatenate([mask] * 3, axis=1), stacked)
    sums_top, sums_middle = pieces(sums, 2)
    outer = dot(
        jnp.concatenate([top, middle, top], axis=0),
        jnp.concatenate([sums_top, sums_top, sums_middle], axis=0),
        0,
        0,
    )
    high, low = pieces(outer + (16.0 * last / root) * gram, 2)
    scale = -inverse * inverse * (1.0 / feat)
    grad_ref[...] = ((dot(high, feats) + dot(low, feats)) * scale).astype(BF16)


def second_kernel(blocks, grad_ref, hid_ref, keep_ref, send_ref, ht_ref):
    split_parity(blocks, hid_ref[...], ht_ref)
    parity = lax.axis_index("gy") % 2
    keep_ref[...] = dot(ht_ref[parity], grad_ref[...])
    send_ref[...] = dot(ht_ref[1 - parity], grad_ref[...]).astype(BF16)


def first_send_kernel(grad_ref, second_ref, pre_ref, xt_ref, send_ref, pgrad_ref):
    step = 256
    parity = lax.axis_index("gy") % 2
    for i in range(0, pre_ref.shape[1], step):
        hidden_grad = dot(grad_ref[...], second_ref[i : i + step, :], 1, 1)
        pre = pre_ref[:, i : i + step]
        sigma = jax.nn.sigmoid(pre)
        pre_grad = (hidden_grad * sigma * (1.0 + pre * (1.0 - sigma))).astype(BF16)
        pgrad_ref[:, i : i + step] = pre_grad
        send_ref[:, i : i + step] = dot(xt_ref[1 - parity], pre_grad).astype(BF16)


def first_keep_kernel(pgrad_ref, xt_ref, keep_ref):
    step = 256
    parity = lax.axis_index("gy") % 2
    for i in range(0, pgrad_ref.shape[1], step):
        keep_ref[:, i : i + step] = dot(xt_ref[parity], pgrad_ref[:, i : i + step])


def split_kernel(group, leading, axis, unit, *refs):
    parts, outs = refs[:-group], refs[-group:]
    place = lax.axis_index(axis) // unit % group
    for d, out in enumerate(outs):
        target = jnp.bitwise_xor(place, d)
        index = (target,) if leading else (slice(None), target)
        total = parts[0][index].astype(F32)
        for part in parts[1:]:
            total = total + part[index].astype(F32)
        out[...] = total.astype(out.dtype)


def split_stage(axis, unit, parts, outer, group, own_rows, leading=False):
    columns = parts[0].shape[-1]
    shape = (*((group, outer) if leading else (outer, group)), own_rows, columns)
    made = (outer, own_rows, columns)
    return pl.pallas_call(
        functools.partial(split_kernel, group, leading, axis, unit),
        out_shape=[jax.ShapeDtypeStruct(made, F32 if d == 0 else BF16) for d in range(group)],
        in_specs=[VMEM] * len(parts),
        out_specs=[VMEM] * group,
        cost_estimate=cost(outer * group * own_rows * columns * 1000),
        compiler_params=PARAMS,
    )(*[part.reshape(shape) for part in parts])


def swap(array, axis, distance):
    count = lax.axis_size(axis)
    return lax.ppermute(array, axis, [(i, i ^ distance) for i in range(count)])


def exchange(parts, axis, unit):
    return [parts[0]] + [swap(parts[d], axis, d * unit) for d in range(1, len(parts))]


def on_device(inputs, first_weight, second_weight, targets, noise_var, assignment):
    gx_count = lax.axis_size("gx")
    gy_count = lax.axis_size("gy")
    devices = gx_count * gy_count
    per_slot = CAP // devices
    rows, din = inputs.shape
    hid, feat = second_weight.shape
    own_rows = din // devices
    if tight(devices):
        sent_shape = packed_shape = (devices, din // 128 * per_slot + per_slot // 2, 128)
    else:
        sent_shape, packed_shape = (CAP, din + 128), (devices, per_slot, din + 128)
    sent = pl.pallas_call(
        functools.partial(dispatch_kernel, devices),
        out_shape=jax.ShapeDtypeStruct(sent_shape, BF16),
        in_specs=[HBM] * 3,
        out_specs=VMEM,
        scratch_shapes=[
            pltpu.VMEM((1, rows), jnp.int32),
            pltpu.VMEM((rows,), BF16),
            pltpu.VMEM((rows, din), BF16),
            pltpu.SemaphoreType.DMA((3,)),
        ],
        cost_estimate=cost(2 * CAP * rows * din),
    )(assignment.reshape(1, rows), targets, inputs)
    got = lax.all_to_all(
        sent.reshape(packed_shape), ("gx", "gy"), split_axis=0, concat_axis=0, tiled=True
    ).reshape(sent_shape)

    half = din // 2
    x, targ, xt = pl.pallas_call(
        functools.partial(unpack_kernel, devices),
        out_shape=[
            jax.ShapeDtypeStruct((CAP, din), BF16),
            jax.ShapeDtypeStruct((CAP, 128), F32),
            jax.ShapeDtypeStruct((2, half, CAP), BF16),
        ],
        in_specs=[VMEM],
        out_specs=[VMEM] * 3,
        cost_estimate=cost(2 * CAP * din * hid),
        compiler_params=PARAMS,
    )(got)
    pre, hidden = pl.pallas_call(
        hidden_kernel,
        out_shape=[jax.ShapeDtypeStruct((CAP, hid), kind) for kind in (F32, BF16)],
        in_specs=[VMEM] * 2,
        out_specs=[VMEM] * 2,
        cost_estimate=cost(2 * CAP * din * hid),
        compiler_params=PARAMS,
    )(x, first_weight)
    grad, loss = pl.pallas_call(
        fit_kernel,
        out_shape=[
            jax.ShapeDtypeStruct((CAP, feat), BF16),
            jax.ShapeDtypeStruct((1, 1), F32),
        ],
        in_specs=[SMEM] + [VMEM] * 3,
        out_specs=[VMEM] * 2,
        scratch_shapes=[
            pltpu.VMEM((CAP, feat), BF16),
            pltpu.VMEM((CAP, CAP), F32),
            pltpu.VMEM((CAP, CAP), F32),
        ],
        cost_estimate=cost(6 * CAP * din * hid),
        compiler_params=PARAMS,
    )(noise_var, hidden, targ, second_weight)

    send1, pre_grad = pl.pallas_call(
        first_send_kernel,
        out_shape=[
            jax.ShapeDtypeStruct((half, hid), BF16),
            jax.ShapeDtypeStruct((CAP, hid), BF16),
        ],
        in_specs=[VMEM] * 4,
        out_specs=[VMEM] * 2,
        cost_estimate=cost(2 * CAP * din * hid * 3),
        compiler_params=PARAMS,
    )(grad, second_weight, pre, xt)
    keep1 = pl.pallas_call(
        first_keep_kernel,
        out_shape=jax.ShapeDtypeStruct((half, hid), F32),
        in_specs=[VMEM] * 2,
        out_specs=VMEM,
        cost_estimate=cost(CAP * din * hid),
        compiler_params=PARAMS,
    )(pre_grad, xt)
    keep1, hidden = lax.optimization_barrier((keep1, hidden))
    keep2, send2 = pl.pallas_call(
        functools.partial(second_kernel, devices),
        out_shape=[jax.ShapeDtypeStruct((hid // 2, feat), kind) for kind in (F32, BF16)],
        in_specs=[VMEM] * 2,
        out_specs=[VMEM] * 2,
        scratch_shapes=[pltpu.VMEM((2, hid // 2, CAP), BF16)],
        cost_estimate=cost(2 * CAP * hid * feat * 2),
        compiler_params=PARAMS,
    )(grad, hidden)

    plane = gy_count // 2

    def by_gy(parts, outer):
        return split_stage("gy", 2, parts, outer, plane, own_rows)

    def by_gx(parts, outer):
        return split_stage("gx", 1, parts, outer, gx_count, own_rows, True)

    def added(parts):
        return sum(part.astype(F32) for part in parts).reshape(own_rows, -1)

    first_parts = [*by_gy([keep1, swap(send1, "gy", 1)], gx_count)]
    first_parts[0], keep2 = lax.optimization_barrier((first_parts[0], keep2))
    first_parts = exchange(first_parts, "gy", 2)
    second_parts = exchange(by_gx([keep2, swap(send2, "gy", 1)], plane), "gx", 1)

    second_parts = [*by_gy(second_parts, 1)]
    first_parts = exchange(by_gx(first_parts, 1), "gx", 1)
    first_parts[1], *second_parts = lax.optimization_barrier((first_parts[1], *second_parts))
    second_parts = exchange(second_parts, "gy", 2)
    second_total = added(second_parts)
    first_total = added(first_parts)
    return (first_total, second_total, loss.reshape(1))


def solution(mesh):
    return jax.shard_map(
        on_device,
        mesh=mesh,
        in_specs=(
            P(("gx", "gy"), None),
            P(),
            P(),
            P(("gx", "gy")),
            P(("gx", "gy")),
            P(("gx", "gy"), None),
        ),
        out_specs=(P(("gx", "gy"), None), P(("gx", "gy"), None), P(("gx", "gy"))),
        check_vma=False,
    )
```

```python
import functools

import jax
import jax.numpy as jnp
from jax import lax
from jax.experimental import pallas as pl
from jax.experimental.pallas import tpu as pltpu
from jax.sharding import PartitionSpec as P

CAP = 512
POWERS = 16
BF16 = jnp.bfloat16
F32 = jnp.float32
VMEM = pl.BlockSpec(memory_space=pltpu.VMEM)
SMEM = pl.BlockSpec(memory_space=pltpu.SMEM)
HBM = pl.BlockSpec(memory_space=pltpu.HBM)
PARAMS = pltpu.CompilerParams(vmem_limit_bytes=24 * 1024 * 1024)


def cost(work):
    return pl.CostEstimate(flops=int(work), bytes_accessed=0, transcendentals=0)


def dot(left, right, left_dim=1, right_dim=0):
    return lax.dot_general(
        left,
        right,
        (((left_dim,), (right_dim,)), ((), ())),
        preferred_element_type=F32,
    )


def iota(shape, dim):
    return lax.broadcasted_iota(jnp.int32, shape, dim)


def dispatch_kernel(
    devices, assign_hbm, targ_hbm, rows_hbm, out_hbm, assign_ref, targ_ref, rows_ref, made_ref, sems, out_sems
):
    copies = [
        pltpu.make_async_copy(source, target, sems.at[i])
        for i, (source, target) in enumerate(
            ((assign_hbm, assign_ref), (targ_hbm, targ_ref), (rows_hbm, rows_ref))
        )
    ]
    for copy in copies:
        copy.start()
    copies[0].wait()
    assign = assign_ref[...]
    count, width = rows_ref.shape
    per_slot = CAP // devices
    onehot = iota((devices, count), 0) == assign
    earlier = (iota((count, count), 0) < iota((count, count), 1)).astype(BF16)
    rank = dot(onehot.astype(BF16), earlier)
    slot = jnp.sum(jnp.where(onehot, rank, 0.0), axis=0, keepdims=True)
    place = assign * per_slot + slot.astype(jnp.int32)
    copies[1].wait()
    targets = targ_ref[...].astype(F32).reshape(1, count)
    copies[2].wait()
    half, share = CAP // 2, made_ref.shape[0] // 2
    written = []
    for h in range(2):
        out_ref = made_ref.at[h * share : (h + 1) * share]
        here = iota((half, count), 0) + h * half == place
        targ = jnp.sum(jnp.where(here, targets, 0.0), axis=1, keepdims=True)
        placed = dot(here.astype(BF16), rows_ref[...]).astype(BF16)
        if tight(devices):
            for i in range(width // 128):
                block = placed[:, i * 128 : (i + 1) * 128].reshape(share, per_slot, 128)
                out_ref[:, i * per_slot : (i + 1) * per_slot, :] = block
            targ = targ.reshape(share, per_slot, 1)
            lane = iota((share, per_slot // 2, 128), 2)
            targ = jnp.where(lane < 64, targ[:, : per_slot // 2], targ[:, per_slot // 2 :])
            out_ref[:, width // 128 * per_slot :, :] = targ.astype(BF16)
        else:
            out_ref[:, :width] = placed
            out_ref[:, width:] = jnp.broadcast_to(targ, (half, 128)).astype(BF16)
        copy = pltpu.make_async_copy(out_ref, out_hbm.at[h * share : (h + 1) * share], out_sems.at[h])
        copy.start()
        written.append(copy)
    for copy in written:
        copy.wait()


def tight(devices):
    return (CAP // devices) % 16 == 0


def unpack_kernel(devices, got_ref, x_ref, targ_ref, xt_ref):
    din = x_ref.shape[1]
    if tight(devices):
        per_slot = CAP // devices
        for i in range(din // 128):
            block = got_ref[:, i * per_slot : (i + 1) * per_slot, :]
            x_ref[:, i * 128 : (i + 1) * 128] = block.reshape(CAP, 128)
        packed = got_ref[:, din // 128 * per_slot :, :].astype(F32)
        lanes = (devices, per_slot // 2, 128)
        parts = [jnp.broadcast_to(packed[:, :, i : i + 1], lanes) for i in (0, 64)]
        targ_ref[...] = jnp.concatenate(parts, axis=1).reshape(CAP, 128)
    else:
        x_ref[...] = got_ref[:, :din]
        targ_ref[...] = got_ref[:, din:].astype(F32)
    split_parity(devices, x_ref[...], xt_ref)


def split_parity(blocks, source, target):
    width = source.shape[1]
    turned = source.T.reshape(blocks // 2, 2, width // blocks, CAP)
    target[0] = turned[:, 0].reshape(width // 2, CAP)
    target[1] = turned[:, 1].reshape(width // 2, CAP)


def pieces(array, count):
    made = []
    for _ in range(count):
        made.append(array.astype(BF16))
        array = array - made[-1].astype(F32)
    return made


def row_to_column(gram, row):
    parts = []
    for start in range(0, CAP, 64):
        product = gram[start : start + 64, :] * row
        folded = sum(product[:, lane : lane + 128] for lane in range(0, CAP, 128))
        parts.append(jnp.sum(folded, axis=1, keepdims=True))
    return jnp.concatenate(parts, axis=0)


def column_to_row(gram, column):
    total = jnp.zeros((8, CAP), F32)
    for start in range(0, CAP, 64):
        product = gram[start : start + 64, :] * column[start : start + 64, :]
        total = total + jnp.sum(product.reshape(8, 8, CAP), axis=0)
    return jnp.sum(total, axis=0, keepdims=True)


def hidden_kernel(x_ref, first_ref, pre_ref, hid_ref):
    step = 256
    for i in range(0, first_ref.shape[1], step):
        pre = dot(x_ref[...], first_ref[:, i : i + step])
        pre_ref[:, i : i + step] = pre
        hid_ref[:, i : i + step] = (pre * jax.nn.sigmoid(pre)).astype(BF16)


def fit_kernel(noise_ref, hid_ref, targ_ref, second_ref, grad_ref, loss_ref, feat_ref, gram_ref, resid_ref):
    feat = second_ref.shape[1]
    step = 256
    for i in range(0, feat, step):
        feat_ref[:, i : i + step] = dot(hid_ref[...], second_ref[:, i : i + step]).astype(BF16)

    feats = feat_ref[...]
    gram_ref[...] = dot(feats, feats, 1, 1) * (1.0 / feat)
    gram = gram_ref[...]
    noise = noise_ref[0]
    squares = sum(
        jnp.sum((gram[i : i + 64, :] * gram[i : i + 64, :]).reshape(8, 8, CAP), axis=0)
        for i in range(0, CAP, 64)
    )
    root = jnp.sqrt(jnp.sum(squares, keepdims=True) + 1e-06)
    theta = root + noise
    inverse = 1.0 / theta
    diagonal = iota((CAP, CAP), 0) == iota((CAP, CAP), 1)
    resid_ref[...] = (jnp.where(diagonal, root, 0.0) - gram) * inverse
    resid = resid_ref

    targ = targ_ref[...]
    column = targ[:, :1]
    lane = iota((CAP, 128), 1)
    sub = iota((POWERS, CAP), 0)
    columns = jnp.where(lane == 0, targ, 0.0)
    row_set = jnp.zeros((POWERS, CAP), F32)
    targ_row = targ.T[:1, :]
    for k in range(1, POWERS - 1):
        if k % 2 == 1:
            row = column_to_row(resid, column)
            row_set = row_set + jnp.where(sub == k, row, 0.0)
        else:
            column = row_to_column(resid, row)
            columns = columns + jnp.where(lane == k, column, 0.0)
    powers = row_set + columns.T[:POWERS, :]
    moments = jnp.sum(powers * targ_row, axis=1, keepdims=True)
    last = jnp.sum(powers[7:8, :] * powers[8:9, :], axis=1, keepdims=True)
    loss_ref[...] = 0.5 * inverse * (jnp.sum(moments, axis=0, keepdims=True) + last)
    mask = (iota((POWERS, POWERS), 0) + iota((POWERS, POWERS), 1) <= POWERS - 2).astype(BF16)
    top, middle, bottom = pieces(powers, 3)
    stacked = jnp.concatenate([top, middle, bottom], axis=0)
    sums = dot(jnp.concatenate([mask] * 3, axis=1), stacked)
    sums_top, sums_middle = pieces(sums, 2)
    outer = dot(
        jnp.concatenate([top, middle, top], axis=0),
        jnp.concatenate([sums_top, sums_top, sums_middle], axis=0),
        0,
        0,
    )
    high, low = pieces(outer + (16.0 * last / root) * gram, 2)
    scale = -inverse * inverse * (1.0 / feat)
    grad_ref[...] = ((dot(high, feats) + dot(low, feats)) * scale).astype(BF16)


def second_kernel(blocks, grad_ref, hid_ref, keep_ref, send_ref, ht_ref):
    split_parity(blocks, hid_ref[...], ht_ref)
    parity = lax.axis_index("gy") % 2
    keep_ref[...] = dot(ht_ref[parity], grad_ref[...])
    send_ref[...] = dot(ht_ref[1 - parity], grad_ref[...]).astype(BF16)


def first_send_kernel(grad_ref, second_ref, pre_ref, xt_ref, send_ref, pgrad_ref):
    step = 256
    parity = lax.axis_index("gy") % 2
    for i in range(0, pre_ref.shape[1], step):
        hidden_grad = dot(grad_ref[...], second_ref[i : i + step, :], 1, 1)
        pre = pre_ref[:, i : i + step]
        sigma = jax.nn.sigmoid(pre)
        pre_grad = (hidden_grad * sigma * (1.0 + pre * (1.0 - sigma))).astype(BF16)
        pgrad_ref[:, i : i + step] = pre_grad
        send_ref[:, i : i + step] = dot(xt_ref[1 - parity], pre_grad).astype(BF16)


def first_keep_kernel(pgrad_ref, xt_ref, keep_ref):
    step = 256
    parity = lax.axis_index("gy") % 2
    for i in range(0, pgrad_ref.shape[1], step):
        keep_ref[:, i : i + step] = dot(xt_ref[parity], pgrad_ref[:, i : i + step])


def split_kernel(group, leading, axis, unit, *refs):
    parts, outs = refs[:-group], refs[-group:]
    place = lax.axis_index(axis) // unit % group
    for d, out in enumerate(outs):
        target = jnp.bitwise_xor(place, d)
        index = (target,) if leading else (slice(None), target)
        total = parts[0][index].astype(F32)
        for part in parts[1:]:
            total = total + part[index].astype(F32)
        out[...] = total.astype(out.dtype)


def split_stage(axis, unit, parts, outer, group, own_rows, leading=False):
    columns = parts[0].shape[-1]
    shape = (*((group, outer) if leading else (outer, group)), own_rows, columns)
    made = (outer, own_rows, columns)
    return pl.pallas_call(
        functools.partial(split_kernel, group, leading, axis, unit),
        out_shape=[jax.ShapeDtypeStruct(made, F32 if d == 0 else BF16) for d in range(group)],
        in_specs=[VMEM] * len(parts),
        out_specs=[VMEM] * group,
        cost_estimate=cost(outer * group * own_rows * columns * 1000),
        compiler_params=PARAMS,
    )(*[part.reshape(shape) for part in parts])


def swap(array, axis, distance):
    count = lax.axis_size(axis)
    return lax.ppermute(array, axis, [(i, i ^ distance) for i in range(count)])


def exchange(parts, axis, unit):
    count = len(parts)
    hops = {d: min(d, count - d) if axis == "gx" else bin(d).count("1") for d in range(1, count)}
    order = sorted(hops, key=hops.get, reverse=True)
    return [parts[0]] + [swap(parts[d], axis, d * unit) for d in order]


def on_device(inputs, first_weight, second_weight, targets, noise_var, assignment):
    gx_count = lax.axis_size("gx")
    gy_count = lax.axis_size("gy")
    devices = gx_count * gy_count
    per_slot = CAP // devices
    rows, din = inputs.shape
    hid, feat = second_weight.shape
    own_rows = din // devices
    if tight(devices):
        sent_shape = packed_shape = (devices, din // 128 * per_slot + per_slot // 2, 128)
    else:
        sent_shape, packed_shape = (CAP, din + 128), (devices, per_slot, din + 128)
    sent = pl.pallas_call(
        functools.partial(dispatch_kernel, devices),
        out_shape=jax.ShapeDtypeStruct(sent_shape, BF16),
        in_specs=[HBM] * 3,
        out_specs=HBM,
        scratch_shapes=[
            pltpu.VMEM((1, rows), jnp.int32),
            pltpu.VMEM((rows,), BF16),
            pltpu.VMEM((rows, din), BF16),
            pltpu.VMEM(sent_shape, BF16),
            pltpu.SemaphoreType.DMA((3,)),
            pltpu.SemaphoreType.DMA((2,)),
        ],
        cost_estimate=cost(2 * CAP * rows * din),
    )(assignment.reshape(1, rows), targets, inputs)
    got = lax.all_to_all(
        sent.reshape(packed_shape), ("gx", "gy"), split_axis=0, concat_axis=0, tiled=True
    ).reshape(sent_shape)

    half = din // 2
    x, targ, xt = pl.pallas_call(
        functools.partial(unpack_kernel, devices),
        out_shape=[
            jax.ShapeDtypeStruct((CAP, din), BF16),
            jax.ShapeDtypeStruct((CAP, 128), F32),
            jax.ShapeDtypeStruct((2, half, CAP), BF16),
        ],
        in_specs=[VMEM],
        out_specs=[VMEM] * 3,
        cost_estimate=cost(2 * CAP * din * hid),
        compiler_params=PARAMS,
    )(got)
    pre, hidden = pl.pallas_call(
        hidden_kernel,
        out_shape=[jax.ShapeDtypeStruct((CAP, hid), kind) for kind in (F32, BF16)],
        in_specs=[VMEM] * 2,
        out_specs=[VMEM] * 2,
        cost_estimate=cost(2 * CAP * din * hid),
        compiler_params=PARAMS,
    )(x, first_weight)
    grad, loss = pl.pallas_call(
        fit_kernel,
        out_shape=[
            jax.ShapeDtypeStruct((CAP, feat), BF16),
            jax.ShapeDtypeStruct((1, 1), F32),
        ],
        in_specs=[SMEM] + [VMEM] * 3,
        out_specs=[VMEM] * 2,
        scratch_shapes=[
            pltpu.VMEM((CAP, feat), BF16),
            pltpu.VMEM((CAP, CAP), F32),
            pltpu.VMEM((CAP, CAP), F32),
        ],
        cost_estimate=cost(6 * CAP * din * hid),
        compiler_params=PARAMS,
    )(noise_var, hidden, targ, second_weight)

    send1, pre_grad = pl.pallas_call(
        first_send_kernel,
        out_shape=[
            jax.ShapeDtypeStruct((half, hid), BF16),
            jax.ShapeDtypeStruct((CAP, hid), BF16),
        ],
        in_specs=[VMEM] * 4,
        out_specs=[VMEM] * 2,
        cost_estimate=cost(2 * CAP * din * hid * 3),
        compiler_params=PARAMS,
    )(grad, second_weight, pre, xt)
    keep1 = pl.pallas_call(
        first_keep_kernel,
        out_shape=jax.ShapeDtypeStruct((half, hid), F32),
        in_specs=[VMEM] * 2,
        out_specs=VMEM,
        cost_estimate=cost(CAP * din * hid),
        compiler_params=PARAMS,
    )(pre_grad, xt)
    keep1, hidden = lax.optimization_barrier((keep1, hidden))
    keep2, send2 = pl.pallas_call(
        functools.partial(second_kernel, devices),
        out_shape=[jax.ShapeDtypeStruct((hid // 2, feat), kind) for kind in (F32, BF16)],
        in_specs=[VMEM] * 2,
        out_specs=[VMEM] * 2,
        scratch_shapes=[pltpu.VMEM((2, hid // 2, CAP), BF16)],
        cost_estimate=cost(2 * CAP * hid * feat * 2),
        compiler_params=PARAMS,
    )(grad, hidden)

    plane = gy_count // 2

    def by_gy(parts, outer):
        return split_stage("gy", 2, parts, outer, plane, own_rows)

    def by_gx(parts, outer):
        return split_stage("gx", 1, parts, outer, gx_count, own_rows, True)

    def added(parts):
        return sum(part.astype(F32) for part in parts).reshape(own_rows, -1)

    first_parts = [*by_gy([keep1, swap(send1, "gy", 1)], gx_count)]
    first_parts[0], keep2 = lax.optimization_barrier((first_parts[0], keep2))
    first_parts = exchange(first_parts, "gy", 2)
    second_parts = exchange(by_gx([keep2, swap(send2, "gy", 1)], plane), "gx", 1)

    second_parts = [*by_gy(second_parts, 1)]
    first_parts = exchange(by_gx(first_parts, 1), "gx", 1)
    first_parts[-2], *second_parts = lax.optimization_barrier((first_parts[-2], *second_parts))
    second_parts = exchange(second_parts, "gy", 2)
    second_total = added(second_parts)
    first_total = added(first_parts)
    return (first_total, second_total, loss.reshape(1))


def solution(mesh):
    return jax.shard_map(
        on_device,
        mesh=mesh,
        in_specs=(
            P(("gx", "gy"), None),
            P(),
            P(),
            P(("gx", "gy")),
            P(("gx", "gy")),
            P(("gx", "gy"), None),
        ),
        out_specs=(P(("gx", "gy"), None), P(("gx", "gy"), None), P(("gx", "gy"))),
        check_vma=False,
    )
```
